128 devices in a mesh: slab: 8 (over z, core), tile: 16 (over y, x).
Axes of the slice: x: 4, y: 4, z: 4, core: 2. Of those that a mesh axis runs over, the one named last changes fastest.
Arguments:
- density: bfloat16 [4096, 128, 128], P(('slab', 'tile')), may hold values from 0.099609375 to 10
- send_list: int32 [128, 16, 4], P(('slab', 'tile')), may hold values from 0 to 31, as said below
- entry_tile: int32 [128, 768], P(('slab', 'tile')), may hold values from 0 to 95
- entry_block: int32 [128, 768], P(('slab', 'tile')), may hold values from 0 to 63
- entry_rows: int32 [128, 768], P(('slab', 'tile')), may hold values from 0 to 63
- entry_cols: int32 [128, 768], P(('slab', 'tile')), may hold values from 0 to 63
- rows_table: bfloat16 [64, 128, 128], replicated, may hold values from 0 to 0.0024871826
- cols_table: bfloat16 [64, 128, 128], replicated, may hold values from 0 to 0.0024871826
- target: float32 [1536, 128, 128], P('tile'), may hold values from 0.5 to 8
Outputs:
- image: float32 [1536, 128, 128], P('tile', 'slab')
- density_grad: float32 [4096, 128, 128], P(('slab', 'tile'))
The draws below stay inside these ranges and needn't reach their ends.
Inputs may be any that keep to these rules, and one draw needn't show every extreme that they name: `send_list`: within one row of 4 numbers (one device, one index along tile) the numbers are all different.
All inputs are finite; a program needn't handle non-finite values.
Results may differ from the reference program's by a relative error of at most 0.0003.
Values may be sent and summed in bfloat16 or wider, within the bound.
No kernel may reach another device: no remote copies, remote signals or barrier semaphores. Data moves between devices by JAX's collectives and lax.ppermute only.
A program may use at most 128 MiB of HBM per device.

```python
import math
import jax
import jax.numpy as jnp
from jax import lax

PIX = 128
CELL = 128
KY = 64
KX = 64
BLK_DEV = 32
SLOT = 4
TILES_DEV = 96
ENTRIES = 768
BLOCKS = 4096
TILES = 1536
N_SLAB = 8
N_TILE = 16
DEVICES = 128


def draw_send_list(key, part):
    keys = jax.random.split(key, N_SLAB * N_TILE * N_TILE)
    rows = jax.vmap(lambda one_key: jax.random.permutation(one_key, BLK_DEV)[:SLOT])(keys)
    return rows.reshape(N_SLAB * N_TILE, N_TILE, SLOT).astype(jnp.int32)


def place_ends(array, own_key, least, top_value):
    dims = array.shape
    index_at = [jax.random.randint(jax.random.fold_in(own_key, axis), (), 0, dims[axis]) for axis in range(len(dims))]
    array = array.at[tuple(index_at)].set(least)
    longest = dims.index(max(dims))
    index_at[longest] = (index_at[longest] + 1) % dims[longest]
    return array.at[tuple(index_at)].set(top_value)


def block_scale(rng, extent, cuts, smallest, high):
    level, own = 1.0, jax.random.fold_in(rng, 6)
    for dim, shards_of in cuts:
        steps = jnp.exp(jax.random.uniform(jax.random.fold_in(own, dim), (shards_of,), jnp.float32, smallest / len(cuts), high / len(cuts)))
        level = level * jnp.repeat(steps, extent[dim] // shards_of).reshape([-1 if axis == dim else 1 for axis in range(len(extent))])
    return level


def setup_inputs(seed: int = 0) -> dict:
    splits = jax.random.split(jax.random.key(seed), 10)
    density = jnp.clip(jnp.exp(math.log(10.0) - 4.609084 * jax.random.uniform(splits[0], (BLOCKS, CELL, CELL), jnp.float32) ** block_scale(splits[0], (BLOCKS, CELL, CELL), ((0, 128),), -0.2, 0.2)), 0.099609375, 10.0).astype(jnp.bfloat16)
    send_list = draw_send_list(jax.random.fold_in(splits[9], 71), 0)
    entry_tile = place_ends(jax.random.randint(splits[2], (DEVICES, ENTRIES), 0, TILES_DEV), jax.random.fold_in(splits[2], 1), 0, TILES_DEV - 1).astype(jnp.int32)
    entry_block = place_ends(jax.random.randint(splits[3], (DEVICES, ENTRIES), 0, N_TILE * SLOT), jax.random.fold_in(splits[3], 1), 0, (N_TILE * SLOT) - 1).astype(jnp.int32)
    entry_rows = place_ends(jax.random.randint(splits[4], (DEVICES, ENTRIES), 0, KY), jax.random.fold_in(splits[4], 1), 0, KY - 1).astype(jnp.int32)
    entry_cols = place_ends(jax.random.randint(splits[5], (DEVICES, ENTRIES), 0, KX), jax.random.fold_in(splits[5], 1), 0, KX - 1).astype(jnp.int32)
    rows_table = jnp.clip(jax.random.uniform(splits[6], (KY, PIX, CELL), jnp.float32, 0.0, 0.0024871826), 0.0, 0.0024871826).astype(jnp.bfloat16)
    cols_table = jnp.clip(jax.random.uniform(splits[7], (KX, CELL, PIX), jnp.float32, 0.0, 0.0024871826), 0.0, 0.0024871826).astype(jnp.bfloat16)
    target = jnp.clip(jnp.exp(math.log(8.0) - 2.7725887 * jax.random.uniform(splits[8], (TILES, PIX, PIX), jnp.float32) ** block_scale(splits[8], (TILES, PIX, PIX), ((0, 16),), -0.2, 0.2)), 0.5, 8.0)
    return dict(density=density, send_list=send_list, entry_tile=entry_tile, entry_block=entry_block, entry_rows=entry_rows, entry_cols=entry_cols, rows_table=rows_table, cols_table=cols_table, target=target)


entry_group = 64

def received_ids(send_list, slab_id, tile_id):
    owners = slab_id * N_TILE + jnp.arange(N_TILE, dtype=jnp.int32)
    local = send_list[owners, tile_id]
    return (owners[:, None] * BLK_DEV + local).reshape(-1).astype(jnp.int32)

def grouped(values, device):
    return values[device].reshape(-1, entry_group)

def device_partial(density, send_list, entry_tile, entry_block, entry_rows, entry_cols, rows_table, cols_table, slab_id, tile_id):
    device = slab_id * N_TILE + tile_id
    received = density[received_ids(send_list, slab_id, tile_id)]

    def forward_step(total, item):
        tile_ids, block_ids, row_ids, col_ids = item
        left = rows_table[row_ids].astype(jnp.float32)
        blocks = received[block_ids].astype(jnp.float32)
        right = cols_table[col_ids].astype(jnp.float32)
        halfway = jnp.einsum('epc,ecd->epd', left, blocks).astype(jnp.bfloat16).astype(jnp.float32)
        contrib = jnp.einsum('epd,edq->epq', halfway, right)
        return (total.at[tile_ids].add(contrib), None)
    start = jnp.zeros((TILES_DEV, PIX, PIX), jnp.float32)
    items = (grouped(entry_tile, device), grouped(entry_block, device), grouped(entry_rows, device), grouped(entry_cols, device))
    total, _ = lax.scan(forward_step, start, items)
    return total

def device_slots(pixel_grad, entry_tile, entry_block, entry_rows, entry_cols, rows_table, cols_table, slab_id, tile_id):
    device = slab_id * N_TILE + tile_id
    own_grad = lax.dynamic_slice_in_dim(pixel_grad, tile_id * TILES_DEV, TILES_DEV, 0)

    def backward_step(total, item):
        tile_ids, block_ids, row_ids, col_ids = item
        left = rows_table[row_ids].astype(jnp.float32)
        right = cols_table[col_ids].astype(jnp.float32)
        grads = own_grad[tile_ids].astype(jnp.float32)
        back = jnp.einsum('epq,edq->epd', grads, right).astype(jnp.bfloat16).astype(jnp.float32)
        delta = jnp.einsum('epc,epd->ecd', left, back)
        return (total.at[block_ids].add(delta), None)
    start = jnp.zeros((N_TILE * SLOT, CELL, CELL), jnp.float32)
    items = (grouped(entry_tile, device), grouped(entry_block, device), grouped(entry_rows, device), grouped(entry_cols, device))
    total, _ = lax.scan(backward_step, start, items)
    return total

def reference(density, send_list, entry_tile, entry_block, entry_rows, entry_cols, rows_table, cols_table, target):
    tile_range = jnp.arange(N_TILE, dtype=jnp.int32)

    def slab_image(total, slab_id):
        parts = lax.map(lambda tile_id: device_partial(density, send_list, entry_tile, entry_block, entry_rows, entry_cols, rows_table, cols_table, slab_id, tile_id), tile_range)
        return (total + parts, None)
    image, _ = lax.scan(slab_image, jnp.zeros((N_TILE, TILES_DEV, PIX, PIX), jnp.float32), jnp.arange(N_SLAB, dtype=jnp.int32))
    image = image.reshape(TILES, PIX, PIX)
    pixel_grad = ((jnp.log1p(image) - jnp.log1p(target)) / (1.0 + image)).astype(jnp.bfloat16)

    def slab_grad(total, slab_id):
        slots = lax.map(lambda tile_id: device_slots(pixel_grad, entry_tile, entry_block, entry_rows, entry_cols, rows_table, cols_table, slab_id, tile_id), tile_range)
        ids = lax.map(lambda tile_id: received_ids(send_list, slab_id, tile_id), tile_range)
        return (total.at[ids.reshape(-1)].add(slots.reshape(-1, CELL, CELL)), None)
    density_grad, _ = lax.scan(slab_grad, jnp.zeros((BLOCKS, CELL, CELL), jnp.float32), jnp.arange(N_SLAB, dtype=jnp.int32))
    return (image, density_grad)
```

```python
import functools
import jax
import jax.numpy as jnp
from jax import lax
from jax.experimental import pallas as pl
from jax.experimental.pallas import tpu as pltpu
from jax.sharding import PartitionSpec as P

bf16, f32, i16, i32 = jnp.bfloat16, jnp.float32, jnp.int16, jnp.int32
vmem_bytes = 56 * 2**20
unroll = 32
top = 32000.0
tiny = 1e-30

SMEM = pl.BlockSpec(memory_space=pltpu.SMEM)
VMEM = pl.BlockSpec(memory_space=pltpu.VMEM)


def params():
    return pltpu.CompilerParams(vmem_limit_bytes=vmem_bytes)


def mm(a, b):
    return jnp.dot(a, b, preferred_element_type=f32)


def code_level(peak):
    return jnp.ceil(8.0 * jnp.log2(jnp.maximum(peak, tiny)))


def forward_kernel(tile_ids, block_ids, row_ids, col_ids, rows, cols, blocks, mine, theirs):
    mine[...] = jnp.zeros_like(mine)
    theirs[...] = jnp.zeros_like(theirs)

    def step(i, carry):
        half = []
        for u in range(unroll):
            e = i * unroll + u
            half.append(mm(rows[row_ids[0, e]], blocks[block_ids[0, e]]).astype(bf16))
        parts = []
        for u in range(unroll):
            e = i * unroll + u
            parts.append(mm(half[u], cols[col_ids[0, e]]))
        for u in range(unroll):
            t = tile_ids[0, i * unroll + u]
            for k in range(4):
                mine[k, t] += parts[u][k * 16:(k + 1) * 16]
                theirs[k, t] += parts[u][64 + k * 16:64 + (k + 1) * 16]
        return carry

    lax.fori_loop(0, tile_ids.shape[1] // unroll, step, 0)


def combine_kernel(mine, got, own, q1, q2, q3):
    own[...] = mine[0] + got[0]
    n = own.shape[0]
    for k, q in ((1, q1), (2, q2), (3, q3)):
        def group(g, carry):
            levels = []
            for s in range(16):
                t = g * 16 + s
                v = mine[k, t] + got[k, t]
                level = code_level(jnp.max(v, axis=0, keepdims=True))
                scale = jnp.exp2(level * -0.125) * (2.0 * top)
                q[t] = jnp.round(v * scale - top).astype(i32).astype(i16)
                levels.append(level)
            q[n + g] = jnp.concatenate(levels, 0).astype(i32).astype(i16)
            return carry
        lax.fori_loop(0, n // 16, group, 0)


def slope_kernel(place, own, q1, q2, q3, target, image, grad):
    n = own.shape[0]

    def group(g, carry):
        steps = [jnp.exp2(q[n + g].astype(i32).astype(f32) * 0.125) * (0.5 / top) for q in (q1, q2, q3)]
        for s in range(16):
            t = g * 16 + s
            v = own[t]
            for q, step in zip((q1, q2, q3), steps):
                v = v + (q[t].astype(i32).astype(f32) + top) * step[s:s + 1]
            image[t] = v
            grad[t] = ((jnp.log1p(v) - jnp.log1p(target[t])) / (1.0 + v)).astype(bf16)
        return carry

    lax.fori_loop(0, n // 16, group, 0)


def backward_kernel(tile_ids, block_ids, row_ids, col_ids, rows_t, cols_t, *rest):
    grads, out, acc = rest[:8], rest[8], rest[9]
    acc[...] = jnp.zeros_like(acc)

    def step(i, carry):
        back = []
        for u in range(unroll):
            e = i * unroll + u
            t = tile_ids[0, e]
            g = jnp.concatenate([band[t] for band in grads], 0)
            back.append(mm(g, cols_t[col_ids[0, e]]).astype(bf16))
        parts = []
        for u in range(unroll):
            parts.append(mm(rows_t[row_ids[0, i * unroll + u]], back[u]))
        for u in range(unroll):
            acc[block_ids[0, i * unroll + u]] += parts[u]
        return carry

    lax.fori_loop(0, tile_ids.shape[1] // unroll, step, 0)
    slots = (out.shape[1] - 16) // 128

    def pack(k, carry):
        levels = []
        for s in range(slots):
            v = acc[k * slots + s]
            level = code_level(jnp.max(jnp.abs(v), axis=0, keepdims=True))
            scale = jnp.exp2(level * -0.125) * top
            out[k, s * 128:(s + 1) * 128] = jnp.round(v * scale).astype(i32).astype(i16)
            levels.append(level)
        levels.append(jnp.zeros((16 - slots, 128), f32))
        out[k, slots * 128:slots * 128 + 16] = jnp.concatenate(levels, 0).astype(i32).astype(i16)
        return carry

    lax.fori_loop(0, out.shape[0], pack, 0)


def scatter_kernel(send, coded, out):
    out[...] = jnp.zeros_like(out)
    slots = (coded.shape[1] - 16) // 128

    def step(k, carry):
        steps = jnp.exp2(coded[k, slots * 128:slots * 128 + 16].astype(i32).astype(f32) * 0.125) * (1.0 / top)
        for s in range(slots):
            v = coded[k, s * 128:(s + 1) * 128].astype(i32).astype(f32) * steps[s:s + 1]
            out[send[k, s]] += v
        return carry

    lax.fori_loop(0, coded.shape[0], step, 0)


def local(density, send_list, entry_tile, entry_block, entry_rows, entry_cols, rows_table, cols_table, target):
    tiles = target.shape[0]
    send = send_list[0]
    peers, slots = send.shape
    me = lax.axis_index("slab")
    depth, core = me // 2, me % 2
    order = ((depth + jnp.arange(4)) % 4)[None, :] * 2 + (core + jnp.arange(2))[:, None] % 2
    order = order.reshape(-1).astype(i32)
    rows = jnp.take(rows_table.reshape(-1, 8, 16, 128), order, axis=1).reshape(rows_table.shape)
    rows_t = jnp.swapaxes(rows, 1, 2)
    cols_t = jnp.swapaxes(cols_table, 1, 2)

    pair = [(i, i ^ 1) for i in range(8)]

    def swap(x):
        return lax.ppermute(x, "slab", pair)

    def along(x, s):
        return lax.ppermute(x, "slab", [(i, (i + 2 * s) % 8) for i in range(8)])

    outgoing = density[send]
    blocks = lax.all_to_all(outgoing, "tile", split_axis=0, concat_axis=0, tiled=True)
    blocks = blocks.reshape(peers * slots, 128, 128)

    bands = jax.ShapeDtypeStruct((4, tiles, 16, 128), f32)
    mine, theirs = pl.pallas_call(
        forward_kernel,
        out_shape=(bands, bands),
        in_specs=[SMEM] * 4 + [VMEM] * 3,
        out_specs=(VMEM, VMEM),
        compiler_params=params(),
    )(entry_tile, entry_block, entry_rows, entry_cols, rows, cols_table, blocks)
    got = swap(theirs)
    coded = jax.ShapeDtypeStruct((tiles + tiles // 16, 16, 128), i16)
    own, q1, q2, q3 = pl.pallas_call(
        combine_kernel,
        out_shape=(jax.ShapeDtypeStruct((tiles, 16, 128), f32), coded, coded, coded),
        in_specs=[VMEM] * 2,
        out_specs=(VMEM,) * 4,
        compiler_params=params(),
    )(mine, got)
    q1, q2, q3 = along(q1, 1), along(q2, 2), along(q3, 3)
    band = pl.BlockSpec((tiles, 16, 128), lambda g, place: (0, 0, 0))
    code = pl.BlockSpec(coded.shape, lambda g, place: (0, 0, 0))
    image, grad = pl.pallas_call(
        slope_kernel,
        out_shape=(jax.ShapeDtypeStruct((tiles, 16, 128), f32), jax.ShapeDtypeStruct((tiles, 16, 128), bf16)),
        grid_spec=pltpu.PrefetchScalarGridSpec(
            num_scalar_prefetch=1,
            grid=(1,),
            in_specs=[band, code, code, code, pl.BlockSpec((tiles, 16, 128), lambda g, place: (0, place[0], 0))],
            out_specs=(band, band),
        ),
        compiler_params=params(),
    )(me.reshape(1).astype(i32), own, q1, q2, q3, target)
    grads = [grad, along(grad, 3), along(grad, 2), along(grad, 1)]
    grads += [swap(g) for g in grads]
    packed = pl.pallas_call(
        backward_kernel,
        out_shape=jax.ShapeDtypeStruct((peers, slots * 128 + 16, 128), i16),
        in_specs=[SMEM] * 4 + [VMEM] * 10,
        out_specs=VMEM,
        scratch_shapes=[pltpu.VMEM((peers * slots, 128, 128), f32)],
        compiler_params=params(),
    )(entry_tile, entry_block, entry_rows, entry_cols, rows_t, cols_t, *grads)
    returned = lax.all_to_all(packed, "tile", split_axis=0, concat_axis=0, tiled=True)
    density_grad = pl.pallas_call(
        scatter_kernel,
        out_shape=jax.ShapeDtypeStruct(density.shape, f32),
        in_specs=[SMEM, VMEM],
        out_specs=VMEM,
        compiler_params=params(),
    )(send, returned)
    return image, density_grad


def solution(mesh):
    return jax.shard_map(
        local,
        mesh=mesh,
        in_specs=(
            P(("slab", "tile"), None, None),
            P(("slab", "tile"), None, None),
            P(("slab", "tile"), None),
            P(("slab", "tile"), None),
            P(("slab", "tile"), None),
            P(("slab", "tile"), None),
            P(),
            P(),
            P("tile", None, None),
        ),
        out_specs=(P("tile", "slab", None), P(("slab", "tile"), None, None)),
        check_vma=False,
    )
```

```python
import functools
import jax
import jax.numpy as jnp
from jax import lax
from jax.experimental import pallas as pl
from jax.experimental.pallas import tpu as pltpu
from jax.sharding import PartitionSpec as P

bf16, f32, i16, i32 = jnp.bfloat16, jnp.float32, jnp.int16, jnp.int32
unroll = 32
groups = 2
top = 32000.0
tiny = 1e-30

SMEM = pl.BlockSpec(memory_space=pltpu.SMEM)
VMEM = pl.BlockSpec(memory_space=pltpu.VMEM)
ANY = pl.BlockSpec(memory_space=pl.ANY)


def params(mib):
    return pltpu.CompilerParams(vmem_limit_bytes=mib * 2**20)


def cost(us):
    return pl.CostEstimate(flops=int(us * 1e10), bytes_accessed=int(us * 3e7), transcendentals=0)


def mm(a, b):
    return jnp.dot(a, b, preferred_element_type=f32)


def code_level(peak):
    return jnp.ceil(8.0 * jnp.log2(jnp.maximum(peak, tiny)))


def gather_kernel(send, density, out):
    for k in range(out.shape[0]):
        for s in range(out.shape[1]):
            out[k, s] = density[send[0, k, s]]


def prepare_kernel(bands, tile_ids, block_ids, row_ids, col_ids, rows_table, cols_table,
                   lists, counts, rows, rows_t, cols_t, *, per):
    count = rows_table.shape[0]
    entries = tile_ids.shape[1]
    stride = lists.shape[1] // groups
    for g in range(groups):
        counts[g] = 0

    def bin_step(i, carry):
        for u in range(16):
            e = i * 16 + u
            tile = tile_ids[0, e]
            g = jnp.int32(0)
            for h in range(1, groups):
                g = g + (tile >= h * per).astype(i32)
            word = (tile - g * per) | (block_ids[0, e] << 7) | (row_ids[0, e] << 13) | (col_ids[0, e] << 20)
            at = counts[g]
            lists[0, g * stride + at] = word
            counts[g] = at + 1
        return carry

    lax.fori_loop(0, entries // 16, bin_step, 0)
    for g in range(groups):
        at = counts[g]

        def pad_step(i, carry):
            lists[0, g * stride + at + i] = jnp.int32(count << 13)
            return carry

        lax.fori_loop(0, unroll, pad_step, 0)

    def table_step(i, carry):
        for u in range(4):
            r = i * 4 + u
            for k in range(8):
                rows[r, k * 16:(k + 1) * 16] = rows_table[r, pl.ds(pl.multiple_of(bands[k] * 16, 16), 16)]
            cols_t[r] = cols_table[r].T
        for u in range(4):
            r = i * 4 + u
            rows_t[r] = rows[r].T
        return carry

    lax.fori_loop(0, count // 4, table_step, 0)
    rows[count] = jnp.zeros(rows.shape[1:], bf16)
    rows_t[count] = jnp.zeros(rows_t.shape[1:], bf16)


def unpack(word):
    return word & 127, (word >> 7) & 63, (word >> 13) & 127, word >> 20


def run_steps(count, step):
    short = (count + unroll - 1) // unroll
    double = short // 2
    lax.fori_loop(0, double, functools.partial(step, width=2 * unroll, first=0), 0)
    lax.fori_loop(0, short - 2 * double, functools.partial(step, width=unroll, first=double * 2 * unroll), 0)


def forward_kernel(lists, counts, rows, cols, blocks, *rest, g):
    mine, theirs = rest[-2:]
    mine[...] = jnp.zeros_like(mine)
    theirs[...] = jnp.zeros_like(theirs)
    base = g * (lists.shape[1] // groups)

    def step(i, carry, width, first):
        items = [unpack(lists[0, base + first + i * width + u]) for u in range(width)]
        half = [mm(rows[r], blocks[b]).astype(bf16) for _, b, r, _ in items]
        parts = [mm(h, cols[c]) for h, (_, _, _, c) in zip(half, items)]
        for part, (t, _, _, _) in zip(parts, items):
            for k in range(4):
                mine[k, t] += part[k * 16:(k + 1) * 16]
                theirs[k, t] += part[64 + k * 16:64 + (k + 1) * 16]
        return carry

    run_steps(counts[g], step)


def combine_kernel(mine, got, *rest):
    own, q1, q2, q3 = rest[-4:]
    own[...] = mine[0] + got[0]
    n = own.shape[0]
    for k, q in ((1, q1), (2, q2), (3, q3)):
        def group(g, carry):
            levels = []
            for s in range(16):
                t = g * 16 + s
                v = mine[k, t] + got[k, t]
                level = code_level(jnp.max(v, axis=0, keepdims=True))
                scale = jnp.exp2(level * -0.125) * (2.0 * top)
                q[t] = jnp.round(v * scale - top).astype(i32).astype(i16)
                levels.append(level)
            q[n + g] = jnp.concatenate(levels, 0).astype(i32).astype(i16)
            return carry
        lax.fori_loop(0, n // 16, group, 0)


def slope_kernel(place, own, q1, q2, q3, target, *rest):
    image, grad = rest[-2:]
    n = own.shape[0]

    def group(g, carry):
        steps = [jnp.exp2(q[n + g].astype(i32).astype(f32) * 0.125) * (0.5 / top) for q in (q1, q2, q3)]
        for s in range(16):
            t = g * 16 + s
            v = own[t]
            for q, step in zip((q1, q2, q3), steps):
                v = v + (q[t].astype(i32).astype(f32) + top) * step[s:s + 1]
            image[t] = v
            grad[t] = ((jnp.log1p(v) - jnp.log1p(target[t])) / (1.0 + v)).astype(bf16)
        return carry

    lax.fori_loop(0, n // 16, group, 0)


def backward_kernel(lists, counts, rows_t, cols_t, *rest, g):
    grads, rest = rest[:8], rest[8:]
    if g:
        rest[-1][...] = rest[0][...]
    else:
        rest[-1][...] = jnp.zeros_like(rest[-1])
    acc = rest[-1]
    base = g * (lists.shape[1] // groups)

    def step(i, carry, width, first):
        items = [unpack(lists[0, base + first + i * width + u]) for u in range(width)]
        back = [
            mm(jnp.concatenate([band[t] for band in grads], 0), cols_t[c]).astype(bf16)
            for t, _, _, c in items
        ]
        parts = [mm(rows_t[r], h) for h, (_, _, r, _) in zip(back, items)]
        for part, (_, b, _, _) in zip(parts, items):
            acc[b] += part
        return carry

    run_steps(counts[g], step)
    if g == groups - 1:
        pack_slots(acc, rest[-2])


def pack_slots(acc, out):
    slots = (out.shape[1] - 16) // 128

    def pack(k, carry):
        levels = []
        for s in range(slots):
            v = acc[k * slots + s]
            level = code_level(jnp.max(jnp.abs(v), axis=0, keepdims=True))
            scale = jnp.exp2(level * -0.125) * top
            out[k, s * 128:(s + 1) * 128] = jnp.round(v * scale).astype(i32).astype(i16)
            levels.append(level)
        levels.append(jnp.zeros((16 - slots, 128), f32))
        out[k, slots * 128:slots * 128 + 16] = jnp.concatenate(levels, 0).astype(i32).astype(i16)
        return carry

    lax.fori_loop(0, out.shape[0], pack, 0)


def scatter_kernel(send, coded, out):
    out[...] = jnp.zeros_like(out)
    slots = (coded.shape[1] - 16) // 128

    def step(k, carry):
        steps = jnp.exp2(coded[k, slots * 128:slots * 128 + 16].astype(i32).astype(f32) * 0.125) * (1.0 / top)
        for s in range(slots):
            v = coded[k, s * 128:(s + 1) * 128].astype(i32).astype(f32) * steps[s:s + 1]
            out[send[0, k, s]] += v
        return carry

    lax.fori_loop(0, coded.shape[0], step, 0)


def local(density, send_list, entry_tile, entry_block, entry_rows, entry_cols, rows_table, cols_table, target):
    tiles = target.shape[0]
    send = send_list
    peers, slots = send.shape[1:]
    me = lax.axis_index("slab")
    depth, core = me // 2, me % 2
    order = ((depth + jnp.arange(4)) % 4)[None, :] * 2 + (core + jnp.arange(2))[:, None] % 2
    order = order.reshape(-1).astype(i32)
    per = tiles // groups

    pair = [(i, i ^ 1) for i in range(8)]

    def swap(x):
        return lax.ppermute(x, "slab", pair)

    def along(x, s):
        return lax.ppermute(x, "slab", [(i, (i + 2 * s) % 8) for i in range(8)])

    outgoing = pl.pallas_call(
        gather_kernel,
        out_shape=jax.ShapeDtypeStruct((peers, slots, 128, 128), bf16),
        in_specs=[SMEM, VMEM],
        out_specs=VMEM,
        compiler_params=params(8),
        cost_estimate=cost(2),
    )(send, density)
    blocks = lax.all_to_all(outgoing, "tile", split_axis=0, concat_axis=0, tiled=True)
    blocks = blocks.reshape(peers * slots, 128, 128)

    table = jax.ShapeDtypeStruct((rows_table.shape[0] + 1, 128, 128), bf16)
    lists, counts, rows, rows_t, cols_t = pl.pallas_call(
        functools.partial(prepare_kernel, per=per),
        out_shape=(
            jax.ShapeDtypeStruct((1, groups * (entry_tile.shape[1] + 128)), i32),
            jax.ShapeDtypeStruct((groups,), i32),
            table,
            table,
            jax.ShapeDtypeStruct(cols_table.shape, bf16),
        ),
        in_specs=[SMEM] * 5 + [VMEM] * 2,
        out_specs=(SMEM, SMEM, VMEM, VMEM, VMEM),
        compiler_params=params(16),
        cost_estimate=cost(15),
    )(order, entry_tile, entry_block, entry_rows, entry_cols, rows_table, cols_table)

    bands = jax.ShapeDtypeStruct((4, per, 16, 128), f32)
    coded = jax.ShapeDtypeStruct((per + per // 16, 16, 128), i16)
    band = pl.BlockSpec((per, 16, 128), lambda i, place: (0, 0, 0))
    code = pl.BlockSpec(coded.shape, lambda i, place: (0, 0, 0))

    def forward(g, after):
        mine, theirs = pl.pallas_call(
            functools.partial(forward_kernel, g=g),
            out_shape=(bands, bands),
            in_specs=[SMEM] * 2 + [VMEM] * 3 + [ANY] * len(after),
            out_specs=(VMEM, VMEM),
            compiler_params=params(16),
            cost_estimate=cost(20 / groups),
        )(lists, counts, rows, cols_table, blocks, *after)
        return mine, swap(theirs)

    def combine(mine, got, after):
        return pl.pallas_call(
            combine_kernel,
            out_shape=(jax.ShapeDtypeStruct((per, 16, 128), f32), coded, coded, coded),
            in_specs=[VMEM] * 2 + [ANY] * len(after),
            out_specs=(VMEM,) * 4,
            compiler_params=params(16),
            cost_estimate=cost(2 / groups),
        )(mine, got, *after)

    def slope(g, part, held):
        return pl.pallas_call(
            slope_kernel,
            out_shape=(jax.ShapeDtypeStruct((tiles, 16, 128), f32), jax.ShapeDtypeStruct((per, 16, 128), bf16)),
            grid_spec=pltpu.PrefetchScalarGridSpec(
                num_scalar_prefetch=1,
                grid=(1,),
                in_specs=[band, code, code, code, pl.BlockSpec((per, 16, 128), lambda i, place, g=g: (g, place[0], 0))]
                + [ANY] * len(held),
                out_specs=(pl.BlockSpec((per, 16, 128), lambda i, place, g=g: (g, 0, 0)), band),
            ),
            input_output_aliases={6: 0} if held else {},
            compiler_params=params(16),
            cost_estimate=cost(3 / groups),
        )(me.reshape(1).astype(i32), *part, target, *held)

    image, token = [], []
    parts, grads = [], []

    def finish(part):
        nonlocal image, token
        picture, grad = slope(len(grads), part, image)
        image, token = [picture], [grad]
        grads.append((grad, along(grad, 3), along(grad, 1), along(grad, 2)))

    for g in range(groups):
        mine, got = forward(g, token)
        if g:
            finish(parts[g - 1])
        own, q1, q2, q3 = combine(mine, got, token if g else [])
        token = [own]
        parts.append((own, along(q1, 1), along(q3, 3), along(q2, 2)))
    finish(parts[-1])
    image = image[0]
    acc = None
    slot_sums = jax.ShapeDtypeStruct((peers * slots, 128, 128), f32)
    packed_shape = jax.ShapeDtypeStruct((peers, slots * 128 + 16, 128), i16)
    for g in range(groups):
        last = g == groups - 1
        near = grads[g]
        if g:
            near, acc = lax.optimization_barrier((near, acc))
        near = [near[0], near[1], near[3], near[2]]
        near = near + [swap(x) for x in near]
        acc = pl.pallas_call(
            functools.partial(backward_kernel, g=g),
            out_shape=packed_shape if last else slot_sums,
            in_specs=[SMEM] * 2 + [VMEM] * (11 if g else 10) + [ANY] * (0 if g else 1),
            out_specs=VMEM,
            scratch_shapes=[pltpu.VMEM(slot_sums.shape, f32)] if last else [],
            compiler_params=params(24),
            cost_estimate=cost(20 / groups),
        )(lists, counts, rows_t, cols_t, *near, *([acc] if g else token))
    returned = lax.all_to_all(acc, "tile", split_axis=0, concat_axis=0, tiled=True)
    density_grad = pl.pallas_call(
        scatter_kernel,
        out_shape=jax.ShapeDtypeStruct(density.shape, f32),
        in_specs=[SMEM, VMEM],
        out_specs=VMEM,
        compiler_params=params(8),
        cost_estimate=cost(4),
    )(send, returned)
    return image, density_grad


def solution(mesh):
    return jax.shard_map(
        local,
        mesh=mesh,
        in_specs=(
            P(("slab", "tile"), None, None),
            P(("slab", "tile"), None, None),
            P(("slab", "tile"), None),
            P(("slab", "tile"), None),
            P(("slab", "tile"), None),
            P(("slab", "tile"), None),
            P(),
            P(),
            P("tile", None, None),
        ),
        out_specs=(P("tile", "slab", None), P(("slab", "tile"), None, None)),
        check_vma=False,
    )
```

```python
import functools
import jax
import jax.numpy as jnp
from jax import lax
from jax.experimental import pallas as pl
from jax.experimental.pallas import tpu as pltpu
from jax.sharding import PartitionSpec as P

bf16, f32, i16, i32 = jnp.bfloat16, jnp.float32, jnp.int16, jnp.int32
unroll = 32
groups = 2
top = 32000.0
tiny = 1e-30

SMEM = pl.BlockSpec(memory_space=pltpu.SMEM)
VMEM = pl.BlockSpec(memory_space=pltpu.VMEM)
ANY = pl.BlockSpec(memory_space=pl.ANY)


def params(mib):
    return pltpu.CompilerParams(vmem_limit_bytes=mib * 2**20)


def cost(us):
    return pl.CostEstimate(flops=int(us * 1e10), bytes_accessed=int(us * 3e7), transcendentals=0)


def mm(a, b):
    return jnp.dot(a, b, preferred_element_type=f32)


def code_level(peak):
    return jnp.ceil(8.0 * jnp.log2(jnp.maximum(peak, tiny)))


def gather_kernel(send, density, out):
    for k in range(out.shape[0]):
        for s in range(out.shape[1]):
            out[k, s] = density[send[0, k, s]]


def prepare_kernel(bands, tile_ids, block_ids, row_ids, col_ids, rows_table, cols_table, after,
                   lists, counts, rows_t, cols_t, *, per):
    count = rows_table.shape[0]
    entries = tile_ids.shape[1]
    stride = lists.shape[1] // groups
    for g in range(groups):
        counts[g] = 0

    def bin_step(i, carry):
        for u in range(16):
            e = i * 16 + u
            tile = tile_ids[0, e]
            g = jnp.int32(0)
            for h in range(1, groups):
                g = g + (tile >= h * per).astype(i32)
            word = (tile - g * per) | (block_ids[0, e] << 7) | (row_ids[0, e] << 13) | (col_ids[0, e] << 20)
            at = counts[g]
            lists[0, g * stride + at] = word
            counts[g] = at + 1
        return carry

    lax.fori_loop(0, entries // 16, bin_step, 0)
    for g in range(groups):
        at = counts[g]

        def pad_step(i, carry):
            lists[0, g * stride + at + i] = jnp.int32(count << 13)
            return carry

        lax.fori_loop(0, unroll, pad_step, 0)

    starts = [pl.multiple_of(bands[k] * 16, 16) for k in range(8)]

    def table_step(i, carry):
        for u in range(4):
            r = i * 4 + u
            cols_t[r] = cols_table[r].T
            rows_t[r] = jnp.concatenate([rows_table[r, pl.ds(start, 16)] for start in starts], 0).T
        return carry

    lax.fori_loop(0, count // 4, table_step, 0)
    rows_t[count] = jnp.zeros(rows_t.shape[1:], bf16)


def unpack(word):
    return word & 127, (word >> 7) & 63, (word >> 13) & 127, word >> 20


def run_steps(count, step):
    short = (count + unroll - 1) // unroll
    double = short // 2
    lax.fori_loop(0, double, functools.partial(step, width=2 * unroll, first=0), 0)
    lax.fori_loop(0, short - 2 * double, functools.partial(step, width=unroll, first=double * 2 * unroll), 0)


def forward_kernel(bands, tile_ids, block_ids, row_ids, col_ids, rows, cols, blocks, *sums):
    for total in sums:
        total[...] = jnp.zeros_like(total)
    starts = [pl.multiple_of(bands[k] * 16, 16) for k in range(8)]

    def step(i, carry):
        entries = [i * 2 * unroll + u for u in range(2 * unroll)]
        half = []
        for e in entries:
            r = row_ids[0, e]
            left = jnp.concatenate([rows[r, pl.ds(start, 16)] for start in starts], 0)
            half.append(mm(left, blocks[block_ids[0, e]]).astype(bf16))
        parts = [mm(h, cols[col_ids[0, e]]) for h, e in zip(half, entries)]
        for part, e in zip(parts, entries):
            t = tile_ids[0, e]
            for k, total in enumerate(sums):
                total[t] += part[k * 16:(k + 1) * 16]
        return carry

    lax.fori_loop(0, tile_ids.shape[1] // (2 * unroll), step, 0)


def combine_kernel(mine, got, q):
    per = mine.shape[0] // groups
    wide = q.shape[0] // groups
    for g in range(groups):
        def pack(h, carry):
            levels = []
            for s in range(16):
                t = h * 16 + s
                v = mine[g * per + t] + got[g * per + t]
                level = code_level(jnp.max(v, axis=0, keepdims=True))
                scale = jnp.exp2(level * -0.125) * (2.0 * top)
                q[g * wide + t] = jnp.round(v * scale - top).astype(i32).astype(i16)
                levels.append(level)
            q[g * wide + per + h] = jnp.concatenate(levels, 0).astype(i32).astype(i16)
            return carry

        lax.fori_loop(0, per // 16, pack, 0)


def slope_kernel(place, mine, got, q1, q2, q3, target, *rest):
    image, grad = rest[-2:]
    n = mine.shape[0]

    def group(g, carry):
        steps = [jnp.exp2(q[n + g].astype(i32).astype(f32) * 0.125) * (0.5 / top) for q in (q1, q2, q3)]
        for s in range(16):
            t = g * 16 + s
            v = mine[t] + got[t]
            for q, step in zip((q1, q2, q3), steps):
                v = v + (q[t].astype(i32).astype(f32) + top) * step[s:s + 1]
            image[t] = v
            grad[t] = ((jnp.log1p(v) - jnp.log1p(target[t])) / (1.0 + v)).astype(bf16)
        return carry

    lax.fori_loop(0, n // 16, group, 0)


def backward_kernel(lists, counts, rows_t, cols_t, *rest, g):
    grads, rest = rest[:8], rest[8:]
    if g:
        rest[-1][...] = rest[0][...]
    else:
        rest[-1][...] = jnp.zeros_like(rest[-1])
    acc = rest[-1]
    base = g * (lists.shape[1] // groups)

    def step(i, carry, width, first):
        items = [unpack(lists[0, base + first + i * width + u]) for u in range(width)]
        back = [
            mm(jnp.concatenate([band[t] for band in grads], 0), cols_t[c]).astype(bf16)
            for t, _, _, c in items
        ]
        parts = [mm(rows_t[r], h) for h, (_, _, r, _) in zip(back, items)]
        for part, (_, b, _, _) in zip(parts, items):
            acc[b] += part
        return carry

    run_steps(counts[g], step)
    if g == groups - 1:
        pack_slots(acc, rest[-2])


def pack_slots(acc, out):
    slots = (out.shape[1] - 16) // 128

    def pack(k, carry):
        levels = []
        for s in range(slots):
            v = acc[k * slots + s]
            level = code_level(jnp.max(jnp.abs(v), axis=0, keepdims=True))
            scale = jnp.exp2(level * -0.125) * top
            out[k, s * 128:(s + 1) * 128] = jnp.round(v * scale).astype(i32).astype(i16)
            levels.append(level)
        levels.append(jnp.zeros((16 - slots, 128), f32))
        out[k, slots * 128:slots * 128 + 16] = jnp.concatenate(levels, 0).astype(i32).astype(i16)
        return carry

    lax.fori_loop(0, out.shape[0], pack, 0)


def scatter_kernel(send, coded, out):
    out[...] = jnp.zeros_like(out)
    slots = (coded.shape[1] - 16) // 128

    def step(k, carry):
        steps = jnp.exp2(coded[k, slots * 128:slots * 128 + 16].astype(i32).astype(f32) * 0.125) * (1.0 / top)
        for s in range(slots):
            v = coded[k, s * 128:(s + 1) * 128].astype(i32).astype(f32) * steps[s:s + 1]
            out[send[0, k, s]] += v
        return carry

    lax.fori_loop(0, coded.shape[0], step, 0)


def band_order(me):
    depth, core = me // 2, me % 2
    order = ((depth + jnp.arange(4)) % 4)[None, :] * 2 + (core + jnp.arange(2))[:, None] % 2
    return order.reshape(-1).astype(i32)


def local(density, send_list, entry_tile, entry_block, entry_rows, entry_cols, rows_table, cols_table, target):
    tiles = target.shape[0]
    send = send_list
    peers, slots = send.shape[1:]
    per = tiles // groups

    pair = [(i, i ^ 1) for i in range(8)]

    def swap(x):
        return lax.ppermute(x, "slab", pair)

    def along(x, s):
        return lax.ppermute(x, "slab", [(i, (i + 2 * s) % 8) for i in range(8)])

    me, send = lax.optimization_barrier((lax.axis_index("slab"), send))
    outgoing = pl.pallas_call(
        gather_kernel,
        out_shape=jax.ShapeDtypeStruct((peers, slots, 128, 128), bf16),
        in_specs=[SMEM, VMEM],
        out_specs=VMEM,
        compiler_params=params(8),
        cost_estimate=cost(2),
    )(send, density)
    blocks = lax.all_to_all(outgoing, "tile", split_axis=0, concat_axis=0, tiled=True)
    blocks = blocks.reshape(peers * slots, 128, 128)
    me, blocks = lax.optimization_barrier((me, blocks))
    order = band_order(me)

    band_sum = jax.ShapeDtypeStruct((tiles, 16, 128), f32)
    wide = per + per // 16
    coded = jax.ShapeDtypeStruct((groups * wide, 16, 128), i16)
    sums = pl.pallas_call(
        forward_kernel,
        out_shape=(band_sum,) * 8,
        in_specs=[SMEM] * 5 + [VMEM] * 3,
        out_specs=(VMEM,) * 8,
        compiler_params=params(16),
        cost_estimate=cost(20),
    )(order, entry_tile, entry_block, entry_rows, entry_cols, rows_table, cols_table, blocks)
    mine = sums[:4]
    got = [None] * 4
    coded_sums = [None] * 4
    for k in (2, 1, 3):
        got[k] = swap(sums[4 + k])
        coded_sums[k] = pl.pallas_call(
            combine_kernel,
            out_shape=coded,
            in_specs=[VMEM] * 2,
            out_specs=VMEM,
            compiler_params=params(12),
            cost_estimate=cost(0.5),
        )(mine[k], got[k])
    got[0] = swap(sums[4])
    arrived = [along(coded_sums[k], k) for k in (1, 3, 2)]
    lists, counts, rows_t, cols_t = pl.pallas_call(
        functools.partial(prepare_kernel, per=per),
        out_shape=(
            jax.ShapeDtypeStruct((1, groups * (entry_tile.shape[1] + 128)), i32),
            jax.ShapeDtypeStruct((groups,), i32),
            jax.ShapeDtypeStruct((rows_table.shape[0] + 1, 128, 128), bf16),
            jax.ShapeDtypeStruct(cols_table.shape, bf16),
        ),
        in_specs=[SMEM] * 5 + [VMEM] * 2 + [ANY],
        out_specs=(SMEM, SMEM, VMEM, VMEM),
        compiler_params=params(12),
        cost_estimate=cost(10),
    )(order, entry_tile, entry_block, entry_rows, entry_cols, rows_table, cols_table, coded_sums[3])
    part = (mine[0], got[0], *arrived)
    image, grads, token = [], [], []
    for g in range(groups):
        band = pl.BlockSpec((per, 16, 128), lambda i, place: (0, 0, 0))
        code = pl.BlockSpec((wide, 16, 128), lambda i, place, g=g: (g, 0, 0))
        picked = pl.BlockSpec((per, 16, 128), lambda i, place, g=g: (g, 0, 0))
        picture, grad = pl.pallas_call(
            slope_kernel,
            out_shape=(jax.ShapeDtypeStruct((tiles, 16, 128), f32), jax.ShapeDtypeStruct((per, 16, 128), bf16)),
            grid_spec=pltpu.PrefetchScalarGridSpec(
                num_scalar_prefetch=1,
                grid=(1,),
                in_specs=[picked, picked, code, code, code, pl.BlockSpec((per, 16, 128), lambda i, place, g=g: (g, place[0], 0))]
                + [ANY] * (len(image) + 1),
                out_specs=(picked, band),
            ),
            input_output_aliases={7: 0} if image else {},
            compiler_params=params(16),
            cost_estimate=cost(3 / groups),
        )(me.reshape(1).astype(i32), *part, target, *image, rows_t)
        image, token = [picture], [grad]
        grads.append((grad, along(grad, 3), along(grad, 1), along(grad, 2)))
    image = image[0]
    acc = None
    slot_sums = jax.ShapeDtypeStruct((peers * slots, 128, 128), f32)
    packed_shape = jax.ShapeDtypeStruct((peers, slots * 128 + 16, 128), i16)
    for g in range(groups):
        last = g == groups - 1
        near = grads[g]
        if g:
            near, acc = lax.optimization_barrier((near, acc))
        else:
            near, token = lax.optimization_barrier((near, token))
        near = [near[0], near[1], near[3], near[2]]
        near = near + [swap(x) for x in near]
        acc = pl.pallas_call(
            functools.partial(backward_kernel, g=g),
            out_shape=packed_shape if last else slot_sums,
            in_specs=[SMEM] * 2 + [VMEM] * (11 if g else 10) + [ANY] * (0 if g else 1),
            out_specs=VMEM,
            scratch_shapes=[pltpu.VMEM(slot_sums.shape, f32)] if last else [],
            compiler_params=params(24),
            cost_estimate=cost(20 / groups),
        )(lists, counts, rows_t, cols_t, *near, *([acc] if g else token))
    returned = lax.all_to_all(acc, "tile", split_axis=0, concat_axis=0, tiled=True)
    density_grad = pl.pallas_call(
        scatter_kernel,
        out_shape=jax.ShapeDtypeStruct(density.shape, f32),
        in_specs=[SMEM, VMEM],
        out_specs=VMEM,
        compiler_params=params(8),
        cost_estimate=cost(4),
    )(send, returned)
    return image, density_grad


def solution(mesh):
    return jax.shard_map(
        local,
        mesh=mesh,
        in_specs=(
            P(("slab", "tile"), None, None),
            P(("slab", "tile"), None, None),
            P(("slab", "tile"), None),
            P(("slab", "tile"), None),
            P(("slab", "tile"), None),
            P(("slab", "tile"), None),
            P(),
            P(),
            P("tile", None, None),
        ),
        out_specs=(P("tile", "slab", None), P(("slab", "tile"), None, None)),
        check_vma=False,
    )
```

```python
import functools
import jax
import jax.numpy as jnp
from jax import lax
from jax.experimental import pallas as pl
from jax.experimental.pallas import tpu as pltpu
from jax.sharding import PartitionSpec as P

bf16, f32, i16, i32 = jnp.bfloat16, jnp.float32, jnp.int16, jnp.int32
unroll = 32
groups = 2
top = 32000.0
tiny = 1e-30

SMEM = pl.BlockSpec(memory_space=pltpu.SMEM)
VMEM = pl.BlockSpec(memory_space=pltpu.VMEM)
ANY = pl.BlockSpec(memory_space=pl.ANY)


def params(mib):
    return pltpu.CompilerParams(vmem_limit_bytes=mib * 2**20)


def cost(us):
    return pl.CostEstimate(flops=int(us * 1e10), bytes_accessed=int(us * 3e7), transcendentals=0)


def mm(a, b):
    return jnp.dot(a, b, preferred_element_type=f32)


def code_level(peak):
    return jnp.ceil(8.0 * jnp.log2(jnp.maximum(peak, tiny)))


def gather_kernel(send, density, out):
    for k in range(out.shape[0]):
        for s in range(out.shape[1]):
            out[k, s] = density[send[0, k, s]]


def prepare_kernel(bands, tile_ids, block_ids, row_ids, col_ids, rows_table, cols_table, after,
                   lists, counts, rows_t, cols_t, *, per):
    count = rows_table.shape[0]
    entries = tile_ids.shape[1]
    stride = lists.shape[1] // groups
    for g in range(groups):
        counts[g] = 0

    def bin_step(i, carry):
        for u in range(16):
            e = i * 16 + u
            tile = tile_ids[0, e]
            g = jnp.int32(0)
            for h in range(1, groups):
                g = g + (tile >= h * per).astype(i32)
            word = (tile - g * per) | (block_ids[0, e] << 7) | (row_ids[0, e] << 13) | (col_ids[0, e] << 20)
            at = counts[g]
            lists[0, g * stride + at] = word
            counts[g] = at + 1
        return carry

    lax.fori_loop(0, entries // 16, bin_step, 0)
    for g in range(groups):
        at = counts[g]

        def pad_step(i, carry):
            lists[0, g * stride + at + i] = jnp.int32(count << 13)
            return carry

        lax.fori_loop(0, unroll, pad_step, 0)

    starts = [pl.multiple_of(bands[k] * 16, 16) for k in range(8)]

    def table_step(i, carry):
        for u in range(4):
            r = i * 4 + u
            cols_t[r] = cols_table[r].T
            rows_t[r] = jnp.concatenate([rows_table[r, pl.ds(start, 16)] for start in starts], 0).T
        return carry

    lax.fori_loop(0, count // 4, table_step, 0)
    rows_t[count] = jnp.zeros(rows_t.shape[1:], bf16)


def unpack(word):
    return word & 127, (word >> 7) & 63, (word >> 13) & 127, word >> 20


def run_steps(count, step):
    short = (count + unroll - 1) // unroll
    double = short // 2
    lax.fori_loop(0, double, functools.partial(step, width=2 * unroll, first=0), 0)
    lax.fori_loop(0, short - 2 * double, functools.partial(step, width=unroll, first=double * 2 * unroll), 0)


def forward_kernel(bands, tile_ids, block_ids, row_ids, col_ids, rows, cols, blocks, *sums):
    for total in sums:
        total[...] = jnp.zeros_like(total)
    starts = [pl.multiple_of(bands[k] * 16, 16) for k in range(8)]

    def step(i, carry):
        entries = [i * 2 * unroll + u for u in range(2 * unroll)]
        half = []
        for e in entries:
            r = row_ids[0, e]
            left = jnp.concatenate([rows[r, pl.ds(start, 16)] for start in starts], 0)
            half.append(mm(left, blocks[block_ids[0, e]]).astype(bf16))
        parts = [mm(h, cols[col_ids[0, e]]) for h, e in zip(half, entries)]
        for part, e in zip(parts, entries):
            t = tile_ids[0, e]
            for k, total in enumerate(sums):
                total[t] += part[k * 16:(k + 1) * 16]
        return carry

    lax.fori_loop(0, tile_ids.shape[1] // (2 * unroll), step, 0)


def combine_kernel(mine, got, q):
    per = mine.shape[0] // groups
    wide = q.shape[0] // groups
    for g in range(groups):
        def pack(h, carry):
            levels = []
            for s in range(16):
                t = h * 16 + s
                v = mine[g * per + t] + got[g * per + t]
                level = code_level(jnp.max(v, axis=0, keepdims=True))
                scale = jnp.exp2(level * -0.125) * (2.0 * top)
                q[g * wide + t] = jnp.round(v * scale - top).astype(i32).astype(i16)
                levels.append(level)
            q[g * wide + per + h] = jnp.concatenate(levels, 0).astype(i32).astype(i16)
            return carry

        lax.fori_loop(0, per // 16, pack, 0)


def slope_kernel(place, mine, got, q1, q2, q3, target, *rest):
    image, grad = rest[-2:]
    n = mine.shape[0]

    def group(g, carry):
        steps = [jnp.exp2(q[n + g].astype(i32).astype(f32) * 0.125) * (0.5 / top) for q in (q1, q2, q3)]
        for s in range(16):
            t = g * 16 + s
            v = mine[t] + got[t]
            for q, step in zip((q1, q2, q3), steps):
                v = v + (q[t].astype(i32).astype(f32) + top) * step[s:s + 1]
            image[t] = v
            grad[t] = ((jnp.log1p(v) - jnp.log1p(target[t])) / (1.0 + v)).astype(bf16)
        return carry

    lax.fori_loop(0, n // 16, group, 0)


def backward_kernel(lists, counts, rows_t, cols_t, *rest, g):
    grads, rest = rest[:8], rest[8:]
    if g:
        rest[-1][...] = rest[0][...]
    else:
        rest[-1][...] = jnp.zeros_like(rest[-1])
    acc = rest[-1]
    base = g * (lists.shape[1] // groups)

    def step(i, carry, width, first):
        items = [unpack(lists[0, base + first + i * width + u]) for u in range(width)]
        back = [
            mm(jnp.concatenate([band[t] for band in grads], 0), cols_t[c]).astype(bf16)
            for t, _, _, c in items
        ]
        parts = [mm(rows_t[r], h) for h, (_, _, r, _) in zip(back, items)]
        for part, (_, b, _, _) in zip(parts, items):
            acc[b] += part
        return carry

    run_steps(counts[g], step)
    if g == groups - 1:
        pack_slots(acc, rest[-2])


def pack_slots(acc, out):
    slots = (out.shape[1] - 16) // 128

    def pack(k, carry):
        levels = []
        for s in range(slots):
            v = acc[k * slots + s]
            level = code_level(jnp.max(jnp.abs(v), axis=0, keepdims=True))
            scale = jnp.exp2(level * -0.125) * top
            out[k, s * 128:(s + 1) * 128] = jnp.round(v * scale).astype(i32).astype(i16)
            levels.append(level)
        levels.append(jnp.zeros((16 - slots, 128), f32))
        out[k, slots * 128:slots * 128 + 16] = jnp.concatenate(levels, 0).astype(i32).astype(i16)
        return carry

    lax.fori_loop(0, out.shape[0], pack, 0)


def scatter_kernel(send, coded, out):
    out[...] = jnp.zeros_like(out)
    slots = (coded.shape[1] - 16) // 128

    def step(k, carry):
        steps = jnp.exp2(coded[k, slots * 128:slots * 128 + 16].astype(i32).astype(f32) * 0.125) * (1.0 / top)
        for s in range(slots):
            v = coded[k, s * 128:(s + 1) * 128].astype(i32).astype(f32) * steps[s:s + 1]
            out[send[0, k, s]] += v
        return carry

    lax.fori_loop(0, coded.shape[0], step, 0)


def band_order(me):
    depth, core = me // 2, me % 2
    order = ((depth + jnp.arange(4)) % 4)[None, :] * 2 + (core + jnp.arange(2))[:, None] % 2
    return order.reshape(-1).astype(i32)


def local(density, send_list, entry_tile, entry_block, entry_rows, entry_cols, rows_table, cols_table, target):
    tiles = target.shape[0]
    send = send_list
    peers, slots = send.shape[1:]
    per = tiles // groups

    pair = [(i, i ^ 1) for i in range(8)]

    def swap(x):
        return lax.ppermute(x, "slab", pair)

    def along(x, s):
        return lax.ppermute(x, "slab", [(i, (i + 2 * s) % 8) for i in range(8)])

    me, send = lax.optimization_barrier((lax.axis_index("slab"), send))
    outgoing = pl.pallas_call(
        gather_kernel,
        out_shape=jax.ShapeDtypeStruct((peers, slots, 128, 128), bf16),
        in_specs=[SMEM, VMEM],
        out_specs=VMEM,
        compiler_params=params(8),
        cost_estimate=cost(2),
    )(send, density)
    blocks = lax.all_to_all(outgoing, "tile", split_axis=0, concat_axis=0, tiled=True)
    blocks = blocks.reshape(peers * slots, 128, 128)
    me, blocks = lax.optimization_barrier((me, blocks))
    order = band_order(me)

    band_sum = jax.ShapeDtypeStruct((tiles, 16, 128), f32)
    wide = per + per // 16
    coded = jax.ShapeDtypeStruct((groups * wide, 16, 128), i16)
    sums = pl.pallas_call(
        forward_kernel,
        out_shape=(band_sum,) * 8,
        in_specs=[SMEM] * 5 + [VMEM] * 3,
        out_specs=(VMEM,) * 8,
        compiler_params=params(16),
        cost_estimate=cost(20),
    )(order, entry_tile, entry_block, entry_rows, entry_cols, rows_table, cols_table, blocks)
    mine = sums[:4]
    got = [None] * 4
    coded_sums = [None] * 4
    for k in (2, 1, 3):
        got[k] = swap(sums[4 + k])
        coded_sums[k] = pl.pallas_call(
            combine_kernel,
            out_shape=coded,
            in_specs=[VMEM] * 2,
            out_specs=VMEM,
            compiler_params=params(12),
            cost_estimate=cost(0.5),
        )(mine[k], got[k])
    got[0] = swap(sums[4])
    arrived = [along(coded_sums[k], k) for k in (1, 3, 2)]
    lists, counts, rows_t, cols_t = pl.pallas_call(
        functools.partial(prepare_kernel, per=per),
        out_shape=(
            jax.ShapeDtypeStruct((1, groups * (entry_tile.shape[1] + 128)), i32),
            jax.ShapeDtypeStruct((groups,), i32),
            jax.ShapeDtypeStruct((rows_table.shape[0] + 1, 128, 128), bf16),
            jax.ShapeDtypeStruct(cols_table.shape, bf16),
        ),
        in_specs=[SMEM] * 5 + [VMEM] * 2 + [ANY],
        out_specs=(SMEM, SMEM, VMEM, VMEM),
        compiler_params=params(12),
        cost_estimate=cost(10),
    )(order, entry_tile, entry_block, entry_rows, entry_cols, rows_table, cols_table, coded_sums[3])
    part = (mine[0], got[0], *arrived)
    image, grads, token = [], [], []
    for g in range(groups):
        band = pl.BlockSpec((per, 16, 128), lambda i, place: (0, 0, 0))
        code = pl.BlockSpec((wide, 16, 128), lambda i, place, g=g: (g, 0, 0))
        picked = pl.BlockSpec((per, 16, 128), lambda i, place, g=g: (g, 0, 0))
        picture, grad = pl.pallas_call(
            slope_kernel,
            out_shape=(jax.ShapeDtypeStruct((tiles, 16, 128), f32), jax.ShapeDtypeStruct((per, 16, 128), bf16)),
            grid_spec=pltpu.PrefetchScalarGridSpec(
                num_scalar_prefetch=1,
                grid=(1,),
                in_specs=[picked, picked, code, code, code, pl.BlockSpec((per, 16, 128), lambda i, place, g=g: (g, place[0], 0))]
                + [ANY] * (len(image) + 1),
                out_specs=(picked, band),
            ),
            input_output_aliases={7: 0} if image else {},
            compiler_params=params(16),
            cost_estimate=cost(3 / groups),
        )(me.reshape(1).astype(i32), *part, target, *image, rows_t)
        image, token = [picture], [grad]
        grads.append((grad, along(grad, 2), along(grad, 3), along(grad, 1)))
    image = image[0]
    acc = None
    slot_sums = jax.ShapeDtypeStruct((peers * slots, 128, 128), f32)
    packed_shape = jax.ShapeDtypeStruct((peers, slots * 128 + 16, 128), i16)
    for g in range(groups):
        last = g == groups - 1
        near = grads[g]
        if g:
            near, acc = lax.optimization_barrier((near, acc))
        else:
            near, token = lax.optimization_barrier((near, token))
        near = [near[0], near[2], near[1], near[3]]
        near = near + [swap(x) for x in near]
        acc = pl.pallas_call(
            functools.partial(backward_kernel, g=g),
            out_shape=packed_shape if last else slot_sums,
            in_specs=[SMEM] * 2 + [VMEM] * (11 if g else 10) + [ANY] * (0 if g else 1),
            out_specs=VMEM,
            scratch_shapes=[pltpu.VMEM(slot_sums.shape, f32)] if last else [],
            compiler_params=params(24),
            cost_estimate=cost(20 / groups),
        )(lists, counts, rows_t, cols_t, *near, *([acc] if g else token))
    returned = lax.all_to_all(acc, "tile", split_axis=0, concat_axis=0, tiled=True)
    density_grad = pl.pallas_call(
        scatter_kernel,
        out_shape=jax.ShapeDtypeStruct(density.shape, f32),
        in_specs=[SMEM, VMEM],
        out_specs=VMEM,
        compiler_params=params(8),
        cost_estimate=cost(4),
    )(send, returned)
    return image, density_grad


def solution(mesh):
    return jax.shard_map(
        local,
        mesh=mesh,
        in_specs=(
            P(("slab", "tile"), None, None),
            P(("slab", "tile"), None, None),
            P(("slab", "tile"), None),
            P(("slab", "tile"), None),
            P(("slab", "tile"), None),
            P(("slab", "tile"), None),
            P(),
            P(),
            P("tile", None, None),
        ),
        out_specs=(P("tile", "slab", None), P(("slab", "tile"), None, None)),
        check_vma=False,
    )
```

```python
import functools
import jax
import jax.numpy as jnp
from jax import lax
from jax.experimental import pallas as pl
from jax.experimental.pallas import tpu as pltpu
from jax.sharding import PartitionSpec as P

bf16, f32, i16, i32 = jnp.bfloat16, jnp.float32, jnp.int16, jnp.int32
unroll = 32
groups = 2
top = 32000.0
tiny = 1e-30

SMEM = pl.BlockSpec(memory_space=pltpu.SMEM)
VMEM = pl.BlockSpec(memory_space=pltpu.VMEM)
ANY = pl.BlockSpec(memory_space=pl.ANY)


def params(mib):
    return pltpu.CompilerParams(vmem_limit_bytes=mib * 2**20)


def cost(us):
    return pl.CostEstimate(flops=int(us * 1e10), bytes_accessed=int(us * 3e7), transcendentals=0)


def mm(a, b):
    return jnp.dot(a, b, preferred_element_type=f32)


def code_level(peak):
    return jnp.ceil(8.0 * jnp.log2(jnp.maximum(peak, tiny)))


def gather_kernel(send, density, out):
    for k in range(out.shape[0]):
        for s in range(out.shape[1]):
            out[k, s] = density[send[0, k, s]]


def prepare_kernel(bands, tile_ids, block_ids, row_ids, col_ids, rows_table, cols_table, after,
                   lists, counts, rows_t, cols_t, *, per):
    count = rows_table.shape[0]
    entries = tile_ids.shape[1]
    stride = lists.shape[1] // groups
    for g in range(groups):
        counts[g] = 0

    def bin_step(i, carry):
        for u in range(16):
            e = i * 16 + u
            tile = tile_ids[0, e]
            g = jnp.int32(0)
            for h in range(1, groups):
                g = g + (tile >= h * per).astype(i32)
            word = (tile - g * per) | (block_ids[0, e] << 7) | (row_ids[0, e] << 13) | (col_ids[0, e] << 20)
            at = counts[g]
            lists[0, g * stride + at] = word
            counts[g] = at + 1
        return carry

    lax.fori_loop(0, entries // 16, bin_step, 0)
    for g in range(groups):
        at = counts[g]

        def pad_step(i, carry):
            lists[0, g * stride + at + i] = jnp.int32(count << 13)
            return carry

        lax.fori_loop(0, unroll, pad_step, 0)

    starts = [pl.multiple_of(bands[k] * 16, 16) for k in range(8)]

    def table_step(i, carry):
        for u in range(4):
            r = i * 4 + u
            cols_t[r] = cols_table[r].T
            rows_t[r] = jnp.concatenate([rows_table[r, pl.ds(start, 16)] for start in starts], 0).T
        return carry

    lax.fori_loop(0, count // 4, table_step, 0)
    rows_t[count] = jnp.zeros(rows_t.shape[1:], bf16)


def unpack(word):
    return word & 127, (word >> 7) & 63, (word >> 13) & 127, word >> 20


def run_steps(count, step):
    short = (count + unroll - 1) // unroll
    double = short // 2
    lax.fori_loop(0, double, functools.partial(step, width=2 * unroll, first=0), 0)
    lax.fori_loop(0, short - 2 * double, functools.partial(step, width=unroll, first=double * 2 * unroll), 0)


def forward_kernel(bands, tile_ids, block_ids, row_ids, col_ids, rows, cols, blocks, *sums):
    for total in sums:
        total[...] = jnp.zeros_like(total)
    starts = [pl.multiple_of(bands[k] * 16, 16) for k in range(8)]

    def step(i, carry):
        entries = [i * 2 * unroll + u for u in range(2 * unroll)]
        half = []
        for e in entries:
            r = row_ids[0, e]
            left = jnp.concatenate([rows[r, pl.ds(start, 16)] for start in starts], 0)
            half.append(mm(left, blocks[block_ids[0, e]]).astype(bf16))
        parts = [mm(h, cols[col_ids[0, e]]) for h, e in zip(half, entries)]
        for part, e in zip(parts, entries):
            t = tile_ids[0, e]
            for k, total in enumerate(sums):
                total[t] += part[k * 16:(k + 1) * 16]
        return carry

    lax.fori_loop(0, tile_ids.shape[1] // (2 * unroll), step, 0)


def combine_kernel(mine, got, q):
    per = mine.shape[0] // groups
    wide = q.shape[0] // groups
    for g in range(groups):
        def pack(h, carry):
            levels = []
            for s in range(16):
                t = h * 16 + s
                v = mine[g * per + t] + got[g * per + t]
                level = code_level(jnp.max(v, axis=0, keepdims=True))
                scale = jnp.exp2(level * -0.125) * (2.0 * top)
                q[g * wide + t] = jnp.round(v * scale - top).astype(i32).astype(i16)
                levels.append(level)
            q[g * wide + per + h] = jnp.concatenate(levels, 0).astype(i32).astype(i16)
            return carry

        lax.fori_loop(0, per // 16, pack, 0)


def slope_kernel(place, mine, got, q1, q2, q3, target, *rest):
    image, grad = rest[-2:]
    n = mine.shape[0]

    def group(g, carry):
        steps = [jnp.exp2(q[n + g].astype(i32).astype(f32) * 0.125) * (0.5 / top) for q in (q1, q2, q3)]
        for s in range(16):
            t = g * 16 + s
            v = mine[t] + got[t]
            for q, step in zip((q1, q2, q3), steps):
                v = v + (q[t].astype(i32).astype(f32) + top) * step[s:s + 1]
            image[t] = v
            grad[t] = ((jnp.log1p(v) - jnp.log1p(target[t])) / (1.0 + v)).astype(bf16)
        return carry

    lax.fori_loop(0, n // 16, group, 0)


def backward_kernel(lists, counts, rows_t, cols_t, *rest, g):
    grads, rest = rest[:8], rest[8:]
    if g:
        rest[-1][...] = rest[0][...]
    else:
        rest[-1][...] = jnp.zeros_like(rest[-1])
    acc = rest[-1]
    base = g * (lists.shape[1] // groups)

    def step(i, carry, width, first):
        items = [unpack(lists[0, base + first + i * width + u]) for u in range(width)]
        back = [
            mm(jnp.concatenate([band[t] for band in grads], 0), cols_t[c]).astype(bf16)
            for t, _, _, c in items
        ]
        parts = [mm(rows_t[r], h) for h, (_, _, r, _) in zip(back, items)]
        for part, (_, b, _, _) in zip(parts, items):
            acc[b] += part
        return carry

    run_steps(counts[g], step)
    if g == groups - 1:
        pack_slots(acc, rest[-2])


def pack_slots(acc, out):
    slots = (out.shape[1] - 16) // 128

    def pack(k, carry):
        levels = []
        for s in range(slots):
            v = acc[k * slots + s]
            level = code_level(jnp.max(jnp.abs(v), axis=0, keepdims=True))
            scale = jnp.exp2(level * -0.125) * top
            out[k, s * 128:(s + 1) * 128] = jnp.round(v * scale).astype(i32).astype(i16)
            levels.append(level)
        levels.append(jnp.zeros((16 - slots, 128), f32))
        out[k, slots * 128:slots * 128 + 16] = jnp.concatenate(levels, 0).astype(i32).astype(i16)
        return carry

    lax.fori_loop(0, out.shape[0], pack, 0)


def scatter_kernel(send, coded, out):
    out[...] = jnp.zeros_like(out)
    slots = (coded.shape[1] - 16) // 128

    def step(k, carry):
        steps = jnp.exp2(coded[k, slots * 128:slots * 128 + 16].astype(i32).astype(f32) * 0.125) * (1.0 / top)
        for s in range(slots):
            v = coded[k, s * 128:(s + 1) * 128].astype(i32).astype(f32) * steps[s:s + 1]
            out[send[0, k, s]] += v
        return carry

    lax.fori_loop(0, coded.shape[0], step, 0)


def band_order(me):
    depth, core = me // 2, me % 2
    order = ((depth + jnp.arange(4)) % 4)[None, :] * 2 + (core + jnp.arange(2))[:, None] % 2
    return order.reshape(-1).astype(i32)


def local(density, send_list, entry_tile, entry_block, entry_rows, entry_cols, rows_table, cols_table, target):
    tiles = target.shape[0]
    send = send_list
    peers, slots = send.shape[1:]
    per = tiles // groups

    pair = [(i, i ^ 1) for i in range(8)]

    def swap(x):
        return lax.ppermute(x, "slab", pair)

    def along(x, s):
        return lax.ppermute(x, "slab", [(i, (i + 2 * s) % 8) for i in range(8)])

    me, send = lax.optimization_barrier((lax.axis_index("slab"), send))
    outgoing = pl.pallas_call(
        gather_kernel,
        out_shape=jax.ShapeDtypeStruct((peers, slots, 128, 128), bf16),
        in_specs=[SMEM, VMEM],
        out_specs=VMEM,
        compiler_params=params(8),
        cost_estimate=cost(2),
    )(send, density)
    blocks = lax.all_to_all(outgoing, "tile", split_axis=0, concat_axis=0, tiled=True)
    blocks = blocks.reshape(peers * slots, 128, 128)
    me, blocks = lax.optimization_barrier((me, blocks))
    order = band_order(me)

    band_sum = jax.ShapeDtypeStruct((tiles, 16, 128), f32)
    wide = per + per // 16
    coded = jax.ShapeDtypeStruct((groups * wide, 16, 128), i16)
    sums = pl.pallas_call(
        forward_kernel,
        out_shape=(band_sum,) * 8,
        in_specs=[SMEM] * 5 + [VMEM] * 3,
        out_specs=(VMEM,) * 8,
        compiler_params=params(16),
        cost_estimate=cost(20),
    )(order, entry_tile, entry_block, entry_rows, entry_cols, rows_table, cols_table, blocks)
    mine = sums[:4]
    got = [None] * 4
    coded_sums = [None] * 4
    for k in (2, 1, 3):
        got[k] = swap(sums[4 + k])
        coded_sums[k] = pl.pallas_call(
            combine_kernel,
            out_shape=coded,
            in_specs=[VMEM] * 2,
            out_specs=VMEM,
            compiler_params=params(12),
            cost_estimate=cost(0.5),
        )(mine[k], got[k])
    got[0] = swap(sums[4])
    arrived = [along(coded_sums[k], k) for k in (1, 3, 2)]
    lists, counts, rows_t, cols_t = pl.pallas_call(
        functools.partial(prepare_kernel, per=per),
        out_shape=(
            jax.ShapeDtypeStruct((1, groups * (entry_tile.shape[1] + 128)), i32),
            jax.ShapeDtypeStruct((groups,), i32),
            jax.ShapeDtypeStruct((rows_table.shape[0] + 1, 128, 128), bf16),
            jax.ShapeDtypeStruct(cols_table.shape, bf16),
        ),
        in_specs=[SMEM] * 5 + [VMEM] * 2 + [ANY],
        out_specs=(SMEM, SMEM, VMEM, VMEM),
        compiler_params=params(12),
        cost_estimate=cost(10),
    )(order, entry_tile, entry_block, entry_rows, entry_cols, rows_table, cols_table, coded_sums[3])
    part = (mine[0], got[0], *arrived)
    image, grads, token = [], [], []
    for g in range(groups):
        band = pl.BlockSpec((per, 16, 128), lambda i, place: (0, 0, 0))
        code = pl.BlockSpec((wide, 16, 128), lambda i, place, g=g: (g, 0, 0))
        picked = pl.BlockSpec((per, 16, 128), lambda i, place, g=g: (g, 0, 0))
        picture, grad = pl.pallas_call(
            slope_kernel,
            out_shape=(jax.ShapeDtypeStruct((tiles, 16, 128), f32), jax.ShapeDtypeStruct((per, 16, 128), bf16)),
            grid_spec=pltpu.PrefetchScalarGridSpec(
                num_scalar_prefetch=1,
                grid=(1,),
                in_specs=[picked, picked, code, code, code, pl.BlockSpec((per, 16, 128), lambda i, place, g=g: (g, place[0], 0))]
                + [ANY] * (len(image) + 1),
                out_specs=(picked, band),
            ),
            input_output_aliases={7: 0} if image else {},
            compiler_params=params(16),
            cost_estimate=cost(3 / groups),
        )(me.reshape(1).astype(i32), *part, target, *image, rows_t)
        image, token = [picture], [grad]
        grads.append((grad, along(grad, 2), along(grad, 3), along(grad, 1)))
    image = image[0]
    acc = None
    slot_sums = jax.ShapeDtypeStruct((peers * slots, 128, 128), f32)
    packed_shape = jax.ShapeDtypeStruct((peers, slots * 128 + 16, 128), i16)
    for g in range(groups):
        last = g == groups - 1
        near = grads[g]
        if g:
            near, acc = lax.optimization_barrier((near, acc))
        else:
            near, token = lax.optimization_barrier((near, token))
        near = [near[0], near[2], near[1], near[3]]
        near = near + [swap(grads[g][0])] + [swap(x) for x in near[1:]]
        acc = pl.pallas_call(
            functools.partial(backward_kernel, g=g),
            out_shape=packed_shape if last else slot_sums,
            in_specs=[SMEM] * 2 + [VMEM] * (11 if g else 10) + [ANY] * (0 if g else 1),
            out_specs=VMEM,
            scratch_shapes=[pltpu.VMEM(slot_sums.shape, f32)] if last else [],
            compiler_params=params(24),
            cost_estimate=cost(20 / groups),
        )(lists, counts, rows_t, cols_t, *near, *([acc] if g else token))
    returned = lax.all_to_all(acc, "tile", split_axis=0, concat_axis=0, tiled=True)
    density_grad = pl.pallas_call(
        scatter_kernel,
        out_shape=jax.ShapeDtypeStruct(density.shape, f32),
        in_specs=[SMEM, VMEM],
        out_specs=VMEM,
        compiler_params=params(8),
        cost_estimate=cost(4),
    )(send, returned)
    return image, density_grad


def solution(mesh):
    return jax.shard_map(
        local,
        mesh=mesh,
        in_specs=(
            P(("slab", "tile"), None, None),
            P(("slab", "tile"), None, None),
            P(("slab", "tile"), None),
            P(("slab", "tile"), None),
            P(("slab", "tile"), None),
            P(("slab", "tile"), None),
            P(),
            P(),
            P("tile", None, None),
        ),
        out_specs=(P("tile", "slab", None), P(("slab", "tile"), None, None)),
        check_vma=False,
    )
```
